512 devices in a mesh: dp: 4 (over y_lo, core), head: 8 (over z), ctx: 16 (over x, y_hi).
Axes of the slice: x: 4, y: 8 (y_hi: 4, y_lo: 2; y = y_hi * 2 + y_lo), z: 8, core: 2. Of those that a mesh axis runs over, the one named last changes fastest.
Arguments:
- slab_order: int32 [128], P('dp'), parts along dimension 0, may hold values from 0 to 31, each once
- doc_ids: int32 [8192], P('dp'), parts along dimension 0, may hold values from 0 to 3, never falling along the last dimension, each value on 1 to 1024 neighbouring positions
- query_first: bfloat16 [8192, 6144], P(('dp', 'ctx'), 'head'), parts along dimension 0, may hold values from -12 to 12
- query_second: bfloat16 [8192, 6144], P(('dp', 'ctx'), 'head'), parts along dimension 0, may hold values from -12 to 12
- shared_keys: bfloat16 [8192, 1024], P(('dp', 'ctx'), 'head'), parts along dimension 0, may hold values from -4 to 4
- shared_values: bfloat16 [8192, 1024], P(('dp', 'ctx'), 'head'), parts along dimension 0, may hold values from -6 to 6
- out_grad_first: bfloat16 [8192, 6144], P(('dp', 'ctx'), 'head'), parts along dimension 0, may hold values from -6 to 6
- out_grad_second: bfloat16 [8192, 6144], P(('dp', 'ctx'), 'head'), parts along dimension 0, may hold values from -6 to 6
Outputs:
- query_grad_first: bfloat16 [8192, 6144], P(('dp', 'ctx'), 'head'), parts along dimension 0
- query_grad_second: bfloat16 [8192, 6144], P(('dp', 'ctx'), 'head'), parts along dimension 0
- key_grad: bfloat16 [8192, 1024], P(('dp', 'ctx'), 'head'), parts along dimension 0
- value_grad: bfloat16 [8192, 1024], P(('dp', 'ctx'), 'head'), parts along dimension 0
The draws below stay inside these ranges and needn't reach their ends.
There are 4 independent parts, one for each index of `dp`. The reference program is written for one: setup_inputs(seed, part) draws one part's arguments, and reference() takes and returns one part's arrays. A program takes and returns all parts, laid end to end along the dimension named above; each array names one. Nothing has to cross between parts.
Inputs may be any that keep to these rules, and one draw needn't show every extreme that they name: `slab_order`: every slab number appears exactly once. `doc_ids`: document numbers never fall along the positions; each of the 4 numbers names one run of 1 to 1024 positions, one run of exactly 1024.
All inputs are finite; a program needn't handle non-finite values.
Results may differ from the reference program's by a relative error of at most 0.034.
Values may be sent and summed in bfloat16 or wider, within the bound.
No kernel may reach another device: no remote copies, remote signals or barrier semaphores. Data moves between devices by JAX's collectives and lax.ppermute only.
A program may use at most 64 MiB of HBM per device.

```python
import math
import jax
import jax.numpy as jnp
import numpy as np
from jax import lax

HD = 128
HQ = 6
ROWS_DEV = 128
KVH = 8
SEQ = 2048
SLABS = 32
DOC_MOST = 1024


def draw_shared_keys(key, part):
    key = jax.random.fold_in(key, 3)
    drawn = jnp.clip(jax.random.normal(key, (SEQ, KVH * HD), jnp.float32), -4.0, 4.0)
    return drawn.astype(jnp.bfloat16)


def draw_query_first(key, part):
    key = jax.random.fold_in(key, 5)
    drawn = jnp.clip(jax.random.normal(key, (SEQ, KVH * HQ * HD), jnp.float32), -4.0, 4.0)
    return drawn.astype(jnp.bfloat16)


def draw_query_second(key, part):
    key = jax.random.fold_in(key, 7)
    drawn = jnp.clip(jax.random.normal(key, (SEQ, KVH * HQ * HD), jnp.float32), -4.0, 4.0)
    return drawn.astype(jnp.bfloat16)


def steps_of(rng, extent, split, smallest, high):
    level, own = 1.0, jax.random.fold_in(rng, 6)
    for dim, shards_of in split:
        steps = jnp.exp(jax.random.uniform(jax.random.fold_in(own, dim), (shards_of,), jnp.float32, smallest / len(split), high / len(split)))
        level = level * jnp.repeat(steps, extent[dim] // shards_of).reshape([-1 if axis == dim else 1 for axis in range(len(extent))])
    return level


def split_up(amount, total, reach, slope):
    weights = [(1 << 20) // math.isqrt(standing ** slope) + 1 for standing in range(2, amount + 1)]
    spare, given = total - reach - (amount - 1), [1] * (amount - 1)
    while spare > 0:
        candidates = [i for i in range(amount - 1) if given[i] < reach]
        pool, left = sum([weights[i] for i in candidates]), spare
        for i in candidates:
            extra = min(reach - given[i], max(1, left * weights[i] // pool), spare)
            given[i] = given[i] + extra
            spare = spare - extra
    return np.array([reach] + given)


def uneven(own_key, count, total, bound, lean):
    if count == 2:
        one = jax.random.randint(own_key, (), max(1, total - bound), min(bound, total - 1) + 1)
        return jnp.stack([one, total - one])
    lengths = jnp.asarray(split_up(count, total, bound, lean), jnp.int32)
    couples = (count - 1) // 2
    giver, taker = lengths[1:1 + 2 * couples:2], lengths[2:2 + 2 * couples:2]
    slack = jnp.minimum(giver - 1, bound - taker)
    shifted = jax.random.randint(jax.random.fold_in(own_key, 1), (couples,), 0, 1 << 20) % (slack + 1)
    lengths = lengths.at[1:1 + 2 * couples:2].set(giver - shifted).at[2:2 + 2 * couples:2].set(taker + shifted)
    return lengths[jax.random.permutation(jax.random.fold_in(own_key, 2), count)]


def noise(stream_key, dims, deviation, reach, split=(), held_as=jnp.bfloat16):
    result = jax.random.normal(stream_key, dims, jnp.float32) * deviation
    if len(split) > 0:
        result = steps_of(stream_key, dims, split, -0.22, 0.18) * result
    return jnp.clip(result, min=-reach, max=reach).astype(held_as)


def setup_inputs(seed: int = 0, part: int = 0) -> dict:
    keys = jax.random.split(jax.random.key(seed), 9)
    part_keys = jax.random.split(jax.random.fold_in(keys[8], part), 9)
    return {
        "slab_order": jax.random.permutation(part_keys[0], SLABS).astype(jnp.int32),
        "doc_ids": jnp.searchsorted(jnp.cumsum(uneven(part_keys[1], 4, SEQ, DOC_MOST, 0)), jnp.arange(SEQ), side="right").astype(jnp.int32),
        "query_first": draw_query_first(jax.random.fold_in(jax.random.fold_in(keys[8], part), 71), part),
        "query_second": draw_query_second(jax.random.fold_in(jax.random.fold_in(keys[8], part), 71), part),
        "shared_keys": draw_shared_keys(jax.random.fold_in(jax.random.fold_in(keys[8], part), 71), part),
        "shared_values": noise(part_keys[5], (SEQ, KVH * HD), 1.0, 6.0, ((0, 16), (1, 8))),
        "out_grad_first": noise(part_keys[6], (SEQ, KVH * HQ * HD), 1.0, 6.0, ((0, 16), (1, 8))),
        "out_grad_second": noise(part_keys[7], (SEQ, KVH * HQ * HD), 1.0, 6.0, ((0, 16), (1, 8))),
    }


MASKED_SCORE = -1e+30

def storage_layout(slab_order, doc_ids):
    slab_rows = SEQ // SLABS
    within = jnp.arange(slab_rows, dtype=jnp.int32)
    positions = (slab_order[:, None] * slab_rows + within[None, :]).reshape(SEQ).astype(jnp.int32)
    documents = jnp.take(doc_ids, positions, axis=0)
    return (positions, documents)

def settle(values_wide):
    return lax.optimization_barrier(values_wide.astype(jnp.bfloat16)).astype(jnp.float32)

def reference(slab_order, doc_ids, query_first, query_second, shared_keys, shared_values, out_grad_first, out_grad_second):
    positions, documents = storage_layout(slab_order, doc_ids)
    softmax_scale = 1.0 / math.sqrt(HD)
    key_heads = shared_keys.astype(jnp.float32).reshape(SEQ, KVH, HD)
    value_heads = shared_values.astype(jnp.float32).reshape(SEQ, KVH, HD)
    layer_pairs = ((query_first, out_grad_first), (query_second, out_grad_second))

    def query_block(carried, block_id):
        key_sum, value_sum = carried
        row_start = block_id * ROWS_DEV
        own_pos = lax.dynamic_slice_in_dim(positions, row_start, ROWS_DEV)
        own_doc = lax.dynamic_slice_in_dim(documents, row_start, ROWS_DEV)
        allowed = (positions[None, :] <= own_pos[:, None]) & (documents[None, :] == own_doc[:, None])
        results = []
        for query_all, grad_all in layer_pairs:
            query_rows = lax.dynamic_slice_in_dim(query_all, row_start, ROWS_DEV).astype(jnp.float32).reshape(ROWS_DEV, KVH, HQ, HD)
            grad_rows = lax.dynamic_slice_in_dim(grad_all, row_start, ROWS_DEV).astype(jnp.float32).reshape(ROWS_DEV, KVH, HQ, HD)
            scores = softmax_scale * jnp.einsum('rghd,ngd->ghrn', query_rows, key_heads)
            masked = jnp.where(allowed, scores, MASKED_SCORE)
            row_top = lax.optimization_barrier(jnp.max(masked, axis=-1, keepdims=True))
            row_total = lax.optimization_barrier(jnp.sum(jnp.where(allowed, jnp.exp(masked - row_top), 0.0), axis=-1, keepdims=True))
            log_total = row_top + jnp.log(row_total)
            weights = jnp.where(allowed, jnp.exp(masked - log_total), 0.0)
            weights_low = settle(weights)
            attended = settle(jnp.einsum('ghrn,ngd->rghd', weights, value_heads, precision=lax.Precision.HIGHEST))
            offsets = jnp.einsum('rghd,rghd->ghr', grad_rows, attended)
            weight_grad = jnp.einsum('rghd,ngd->ghrn', grad_rows, value_heads)
            score_grad = settle(weights * (weight_grad - offsets[..., None]))
            query_grad = softmax_scale * jnp.einsum('ghrn,ngd->rghd', score_grad, key_heads)
            results.append(query_grad.reshape(ROWS_DEV, KVH * HQ * HD).astype(jnp.bfloat16))
            key_sum = key_sum + softmax_scale * jnp.einsum('ghrn,rghd->ngd', score_grad, query_rows)
            value_sum = value_sum + jnp.einsum('ghrn,rghd->ngd', weights_low, grad_rows)
        return ((key_sum, value_sum), (results[0], results[1]))
    initial = (jnp.zeros((SEQ, KVH, HD), jnp.float32), jnp.zeros((SEQ, KVH, HD), jnp.float32))
    block_ids = jnp.arange(SEQ // ROWS_DEV, dtype=jnp.int32)
    (key_sum, value_sum), (first_blocks, second_blocks) = lax.scan(query_block, initial, block_ids)
    query_grad_first = first_blocks.reshape(SEQ, KVH * HQ * HD)
    query_grad_second = second_blocks.reshape(SEQ, KVH * HQ * HD)
    key_grad = key_sum.reshape(SEQ, KVH * HD).astype(jnp.bfloat16)
    value_grad = value_sum.reshape(SEQ, KVH * HD).astype(jnp.bfloat16)
    return (query_grad_first, query_grad_second, key_grad, value_grad)
```

```python
import functools
import math

import jax
import jax.numpy as jnp
from jax import lax
from jax.experimental import pallas as pl
from jax.experimental.pallas import tpu as pltpu
from jax.sharding import PartitionSpec as P

HD = 128
TILE = 256
COLS = 256
MASKED_SCORE = -1e30
NT = (((1,), (1,)), ((), ()))
NN = (((1,), (0,)), ((), ()))


def dot(left, right, dims):
    return lax.dot_general(left, right, dims, preferred_element_type=jnp.float32)


def attention_kernel(
    order_ref,
    doc_ref,
    q_first,
    q_second,
    g_first,
    g_second,
    kv_ref,
    dq_first,
    dq_second,
    kvg_ref,
    kv_sorted,
    q_rows,
    g_rows,
    scores_ref,
    grads_ref,
    key_sum,
    dq_sum,
):
    slabs = order_ref.shape[0]
    total = kv_ref.shape[0]
    slab = total // slabs
    own = q_first.shape[0] // slab
    heads = q_first.shape[1] // HD
    width = 2 * heads * slab
    first_slab = lax.axis_index("ctx") * own
    scale = 1.0 / math.sqrt(HD)
    scale2 = scale * math.log2(math.e)

    def to_sequence(i, carried):
        at = pl.multiple_of(order_ref[i] * slab, slab)
        kv_sorted[pl.ds(at, slab), :] = kv_ref[pl.ds(pl.multiple_of(i * slab, slab), slab), :]
        return carried

    lax.fori_loop(0, slabs, to_sequence, 0)
    kv_sorted[total:, :] = jnp.zeros((kv_sorted.shape[0] - total, 2 * HD), jnp.bfloat16)
    key_sum[...] = jnp.zeros_like(key_sum)

    for mine in range(own):
        rows = slice(mine * slab, (mine + 1) * slab)
        for layer, (q_ref, g_ref) in enumerate(((q_first, g_first), (q_second, g_second))):
            for head in range(heads):
                at = (layer * heads + head) * slab
                cols = slice(head * HD, (head + 1) * HD)
                q_rows[mine, at : at + slab, :] = q_ref[rows, cols]
                g_rows[mine, at : at + slab, :] = g_ref[rows, cols]

    docs = doc_ref[...]
    bounds = [jnp.sum((docs < d).astype(jnp.int32)) for d in (1, 2, 3)]

    def one_slab(mine, carried):
        pos0 = order_ref[first_slab + mine] * slab
        row_pos = pos0 + (lax.broadcasted_iota(jnp.int32, (1, HD), 1) & (slab - 1))
        row_doc = jnp.zeros((1, HD), jnp.int32)
        low = jnp.int32(0)
        for bound in bounds:
            row_doc = jnp.where(row_pos >= bound, bound, row_doc)
            low = jnp.where(pos0 >= bound, bound, low)
        low = (low // slab) * slab
        tiles = (pos0 + slab - low + (TILE - 1)) // TILE

        def forward(t, state):
            base = pl.multiple_of(low + t * TILE, slab)
            key_pos = base + lax.broadcasted_iota(jnp.int32, (TILE, HD), 0)
            allowed = (key_pos <= row_pos) & (key_pos >= row_doc)
            allowed = jnp.concatenate([allowed] * (COLS // HD), axis=1)
            keys = kv_sorted[pl.ds(base, TILE), :HD]
            values = kv_sorted[pl.ds(base, TILE), HD:]
            new = []
            for block, (top, norm, weighted) in enumerate(state):
                cols = slice(block * COLS, (block + 1) * COLS)
                s = dot(keys, q_rows[mine, cols, :], NT)
                s = jnp.where(allowed, s, MASKED_SCORE)
                scores_ref[t, :, cols] = s
                dp = dot(values, g_rows[mine, cols, :], NT)
                grads_ref[t, :, cols] = dp
                new_top = jnp.maximum(top, jnp.max(s, axis=0, keepdims=True))
                e = jnp.exp2((s - new_top) * scale2)
                fix = jnp.exp2((top - new_top) * scale2)
                norm = norm * fix + jnp.sum(e, axis=0, keepdims=True)
                weighted = weighted * fix + jnp.sum(e * dp, axis=0, keepdims=True)
                new.append((new_top, norm, weighted))
            return tuple(new)

        start = (
            jnp.full((1, COLS), MASKED_SCORE, jnp.float32),
            jnp.zeros((1, COLS), jnp.float32),
            jnp.zeros((1, COLS), jnp.float32),
        )
        state = lax.fori_loop(0, tiles, forward, (start,) * (width // COLS))
        stats = [
            (top * scale2 + jnp.log2(norm), weighted / norm) for (top, norm, weighted) in state
        ]
        dq_sum[...] = jnp.zeros_like(dq_sum)

        def backward(t, carried):
            base = pl.multiple_of(low + t * TILE, slab)
            keys_t = kv_sorted[pl.ds(base, TILE), :HD].T
            dk = jnp.zeros((TILE, HD), jnp.float32)
            dv = jnp.zeros((TILE, HD), jnp.float32)
            for block, (lse, delta) in enumerate(stats):
                cols = slice(block * COLS, (block + 1) * COLS)
                p = jnp.exp2(scores_ref[t, :, cols] * scale2 - lse)
                ds = (p * (grads_ref[t, :, cols] - delta)).astype(jnp.bfloat16)
                dv = dv + dot(p.astype(jnp.bfloat16), g_rows[mine, cols, :], NN)
                dk = dk + dot(ds, q_rows[mine, cols, :], NN)
                dq_sum[:, cols] += dot(keys_t, ds, NN)
            key_sum[pl.ds(base, TILE), :HD] += dk * scale
            key_sum[pl.ds(base, TILE), HD:] += dv
            return carried

        lax.fori_loop(0, tiles, backward, 0)
        dq = (dq_sum[...] * scale).T.astype(jnp.bfloat16)
        rows = pl.ds(pl.multiple_of(mine * slab, slab), slab)
        for layer, out in enumerate((dq_first, dq_second)):
            for head in range(heads):
                at = (layer * heads + head) * slab
                out[rows, head * HD : (head + 1) * HD] = dq[at : at + slab, :]
        return carried

    lax.fori_loop(0, own, one_slab, 0)

    def to_storage(i, carried):
        at = pl.multiple_of(order_ref[i] * slab, slab)
        to = pl.ds(pl.multiple_of(i * slab, slab), slab)
        kvg_ref[to, :] = key_sum[pl.ds(at, slab), :].astype(jnp.bfloat16)
        return carried

    lax.fori_loop(0, slabs, to_storage, 0)


def attention(slab_order, doc_ids, q_first, q_second, g_first, g_second, kv):
    rows, width = q_first.shape
    total = kv.shape[0]
    slab = total // slab_order.shape[0]
    own = rows // slab
    cols = 2 * (width // HD) * slab
    most = -(-(total // 2 + slab) // TILE)
    vmem = pl.BlockSpec(memory_space=pltpu.VMEM)
    return pl.pallas_call(
        attention_kernel,
        out_shape=(
            jax.ShapeDtypeStruct((rows, width), jnp.bfloat16),
            jax.ShapeDtypeStruct((rows, width), jnp.bfloat16),
            jax.ShapeDtypeStruct((total, 2 * HD), jnp.bfloat16),
        ),
        in_specs=[pl.BlockSpec(memory_space=pltpu.SMEM)] + [vmem] * 6,
        out_specs=(vmem,) * 3,
        scratch_shapes=[
            pltpu.VMEM((total + TILE, 2 * HD), jnp.bfloat16),
            pltpu.VMEM((own, cols, HD), jnp.bfloat16),
            pltpu.VMEM((own, cols, HD), jnp.bfloat16),
            pltpu.VMEM((most, TILE, cols), jnp.float32),
            pltpu.VMEM((most, TILE, cols), jnp.float32),
            pltpu.VMEM((total + TILE, 2 * HD), jnp.float32),
            pltpu.VMEM((HD, cols), jnp.float32),
        ],
        compiler_params=pltpu.CompilerParams(vmem_limit_bytes=40 * 1024 * 1024),
    )(slab_order, doc_ids.reshape(-1, HD), q_first, q_second, g_first, g_second, kv)


SIDE = 4
ALONG_X = [[x * SIDE + y for x in range(SIDE)] for y in range(SIDE)]
ALONG_Y = [[x * SIDE + y for y in range(SIDE)] for x in range(SIDE)]


def exchange(blocks, groups):
    return lax.all_to_all(blocks, "ctx", 0, 0, axis_index_groups=groups)


def spread(block, groups):
    copies = jnp.broadcast_to(block[None], (SIDE,) + block.shape)
    return exchange(copies, groups).reshape(SIDE * block.shape[0], block.shape[1])


def collect(terms, groups):
    parts = exchange(terms.reshape(SIDE, -1, terms.shape[1]), groups)
    return jnp.sum(parts.astype(jnp.float32), axis=0).astype(jnp.bfloat16)


def per_device(
    slab_order,
    doc_ids,
    query_first,
    query_second,
    shared_keys,
    shared_values,
    out_grad_first,
    out_grad_second,
):
    kv = jnp.concatenate([shared_keys, shared_values], axis=1)
    kv = spread(spread(kv, ALONG_Y), ALONG_X)
    dq_first, dq_second, terms = attention(
        slab_order, doc_ids, query_first, query_second, out_grad_first, out_grad_second, kv
    )
    summed = collect(collect(terms, ALONG_X), ALONG_Y)
    return (dq_first, dq_second, summed[:, :HD], summed[:, HD:])


def solution(mesh):
    rows = P(("dp", "ctx"), "head")
    return jax.shard_map(
        per_device,
        mesh=mesh,
        in_specs=(P("dp"), P("dp")) + (rows,) * 6,
        out_specs=(rows,) * 4,
        check_vma=False,
    )
```

```python
import functools
import math

import jax
import jax.numpy as jnp
from jax import lax
from jax.experimental import pallas as pl
from jax.experimental.pallas import tpu as pltpu
from jax.sharding import PartitionSpec as P

HD = 128
TILE = 256
COLS = 256
MASKED_SCORE = -1e30
NT = (((1,), (1,)), ((), ()))
NN = (((1,), (0,)), ((), ()))


def dot(left, right, dims):
    return lax.dot_general(left, right, dims, preferred_element_type=jnp.float32)


def attention_kernel(
    order_ref,
    doc_ref,
    q_first,
    q_second,
    g_first,
    g_second,
    kv_ref,
    dq_first,
    dq_second,
    kvg_ref,
    kv_sorted,
    q_rows,
    g_rows,
    scores_ref,
    grads_ref,
    key_sum,
    dq_sum,
):
    slabs = order_ref.shape[0]
    total = kv_ref.shape[0]
    slab = total // slabs
    own = q_first.shape[0] // slab
    heads = q_first.shape[1] // HD
    width = 2 * heads * slab
    first_slab = lax.axis_index("ctx") * own
    scale = 1.0 / math.sqrt(HD)
    scale2 = scale * math.log2(math.e)

    def to_sequence(i, carried):
        at = pl.multiple_of(order_ref[i] * slab, slab)
        kv_sorted[pl.ds(at, slab), :] = kv_ref[pl.ds(pl.multiple_of(i * slab, slab), slab), :]
        return carried

    lax.fori_loop(0, slabs, to_sequence, 0)
    kv_sorted[total:, :] = jnp.zeros((kv_sorted.shape[0] - total, 2 * HD), jnp.bfloat16)
    key_sum[...] = jnp.zeros_like(key_sum)

    for mine in range(own):
        rows = slice(mine * slab, (mine + 1) * slab)
        for layer, (q_ref, g_ref) in enumerate(((q_first, g_first), (q_second, g_second))):
            for head in range(heads):
                at = (layer * heads + head) * slab
                cols = slice(head * HD, (head + 1) * HD)
                q_rows[mine, at : at + slab, :] = q_ref[rows, cols]
                g_rows[mine, at : at + slab, :] = g_ref[rows, cols]

    docs = doc_ref[...]
    bounds = [jnp.sum((docs < d).astype(jnp.int32)) for d in (1, 2, 3)]

    def one_slab(mine, carried):
        pos0 = order_ref[first_slab + mine] * slab
        row_pos = pos0 + (lax.broadcasted_iota(jnp.int32, (1, HD), 1) & (slab - 1))
        row_doc = jnp.zeros((1, HD), jnp.int32)
        low = jnp.int32(0)
        for bound in bounds:
            row_doc = jnp.where(row_pos >= bound, bound, row_doc)
            low = jnp.where(pos0 >= bound, bound, low)
        low = (low // slab) * slab
        tiles = (pos0 + slab - low + (TILE - 1)) // TILE

        def forward(t, state):
            base = pl.multiple_of(low + t * TILE, slab)
            key_pos = base + lax.broadcasted_iota(jnp.int32, (TILE, HD), 0)
            allowed = (key_pos <= row_pos) & (key_pos >= row_doc)
            allowed = jnp.concatenate([allowed] * (COLS // HD), axis=1)
            keys = kv_sorted[pl.ds(base, TILE), :HD]
            values = kv_sorted[pl.ds(base, TILE), HD:]
            new = []
            for block, (top, norm, weighted) in enumerate(state):
                cols = slice(block * COLS, (block + 1) * COLS)
                s = dot(keys, q_rows[mine, cols, :], NT)
                s = jnp.where(allowed, s, MASKED_SCORE)
                scores_ref[t, :, cols] = s
                dp = dot(values, g_rows[mine, cols, :], NT)
                grads_ref[t, :, cols] = dp
                new_top = jnp.maximum(top, jnp.max(s, axis=0, keepdims=True))
                e = jnp.exp2((s - new_top) * scale2)
                fix = jnp.exp2((top - new_top) * scale2)
                norm = norm * fix + jnp.sum(e, axis=0, keepdims=True)
                weighted = weighted * fix + jnp.sum(e * dp, axis=0, keepdims=True)
                new.append((new_top, norm, weighted))
            return tuple(new)

        start = (
            jnp.full((1, COLS), MASKED_SCORE, jnp.float32),
            jnp.zeros((1, COLS), jnp.float32),
            jnp.zeros((1, COLS), jnp.float32),
        )
        state = lax.fori_loop(0, tiles, forward, (start,) * (width // COLS))
        stats = [
            (top * scale2 + jnp.log2(norm), weighted / norm) for (top, norm, weighted) in state
        ]
        dq_sum[...] = jnp.zeros_like(dq_sum)

        def backward(t, carried):
            base = pl.multiple_of(low + t * TILE, slab)
            keys_t = kv_sorted[pl.ds(base, TILE), :HD].T
            dk = jnp.zeros((TILE, HD), jnp.float32)
            dv = jnp.zeros((TILE, HD), jnp.float32)
            for block, (lse, delta) in enumerate(stats):
                cols = slice(block * COLS, (block + 1) * COLS)
                p = jnp.exp2(scores_ref[t, :, cols] * scale2 - lse)
                ds = (p * (grads_ref[t, :, cols] - delta)).astype(jnp.bfloat16)
                dv = dv + dot(p.astype(jnp.bfloat16), g_rows[mine, cols, :], NN)
                dk = dk + dot(ds, q_rows[mine, cols, :], NN)
                dq_sum[:, cols] += dot(keys_t, ds, NN)
            key_sum[pl.ds(base, TILE), :HD] += dk * scale
            key_sum[pl.ds(base, TILE), HD:] += dv
            return carried

        lax.fori_loop(0, tiles, backward, 0)
        dq = (dq_sum[...] * scale).T.astype(jnp.bfloat16)
        rows = pl.ds(pl.multiple_of(mine * slab, slab), slab)
        for layer, out in enumerate((dq_first, dq_second)):
            for head in range(heads):
                at = (layer * heads + head) * slab
                out[rows, head * HD : (head + 1) * HD] = dq[at : at + slab, :]
        return carried

    lax.fori_loop(0, own, one_slab, 0)

    def to_storage(i, carried):
        at = pl.multiple_of(order_ref[i] * slab, slab)
        to = pl.ds(pl.multiple_of(i * slab, slab), slab)
        kvg_ref[to, :] = key_sum[pl.ds(at, slab), :].astype(jnp.bfloat16)
        return carried

    lax.fori_loop(0, slabs, to_storage, 0)


def attention(slab_order, doc_ids, q_first, q_second, g_first, g_second, kv):
    rows, width = q_first.shape
    total = kv.shape[0]
    slab = total // slab_order.shape[0]
    own = rows // slab
    cols = 2 * (width // HD) * slab
    most = -(-(total // 2 + slab) // TILE)
    vmem = pl.BlockSpec(memory_space=pltpu.VMEM)
    return pl.pallas_call(
        attention_kernel,
        out_shape=(
            jax.ShapeDtypeStruct((rows, width), jnp.bfloat16),
            jax.ShapeDtypeStruct((rows, width), jnp.bfloat16),
            jax.ShapeDtypeStruct((total, 2 * HD), jnp.bfloat16),
        ),
        in_specs=[pl.BlockSpec(memory_space=pltpu.SMEM)] + [vmem] * 6,
        out_specs=(vmem,) * 3,
        scratch_shapes=[
            pltpu.VMEM((total + TILE, 2 * HD), jnp.bfloat16),
            pltpu.VMEM((own, cols, HD), jnp.bfloat16),
            pltpu.VMEM((own, cols, HD), jnp.bfloat16),
            pltpu.VMEM((most, TILE, cols), jnp.float32),
            pltpu.VMEM((most, TILE, cols), jnp.float32),
            pltpu.VMEM((total + TILE, 2 * HD), jnp.float32),
            pltpu.VMEM((HD, cols), jnp.float32),
        ],
        compiler_params=pltpu.CompilerParams(vmem_limit_bytes=40 * 1024 * 1024),
    )(slab_order, doc_ids.reshape(-1, HD), q_first, q_second, g_first, g_second, kv)


def exchange(blocks):
    return lax.all_to_all(blocks, "ctx", 0, 0)


def per_device(
    slab_order,
    doc_ids,
    query_first,
    query_second,
    shared_keys,
    shared_values,
    out_grad_first,
    out_grad_second,
):
    peers = lax.axis_size("ctx")
    kv = jnp.concatenate([shared_keys, shared_values], axis=1)
    kv = exchange(jnp.broadcast_to(kv[None], (peers,) + kv.shape)).reshape(-1, 2 * HD)
    dq_first, dq_second, terms = attention(
        slab_order, doc_ids, query_first, query_second, out_grad_first, out_grad_second, kv
    )
    parts = exchange(terms.reshape(peers, -1, 2 * HD))
    dk = jnp.sum(parts[:, :, :HD].astype(jnp.float32), axis=0).astype(jnp.bfloat16)
    dv = jnp.sum(parts[:, :, HD:].astype(jnp.float32), axis=0).astype(jnp.bfloat16)
    return (dq_first, dq_second, dk, dv)


def solution(mesh):
    rows = P(("dp", "ctx"), "head")
    return jax.shard_map(
        per_device,
        mesh=mesh,
        in_specs=(P("dp"), P("dp")) + (rows,) * 6,
        out_specs=(rows,) * 4,
        check_vma=False,
    )
```

```python
import functools
import math

import jax
import jax.numpy as jnp
from jax import lax
from jax.experimental import pallas as pl
from jax.experimental.pallas import tpu as pltpu
from jax.sharding import PartitionSpec as P

HD = 128
SIZES = (256, 512, 768, 1024, 1152)
CHUNK = 512
FACTS = 48
MASKED_SCORE = -1e30
NT = (((1,), (1,)), ((), ()))
NN = (((1,), (0,)), ((), ()))


def dot(left, right, dims):
    return lax.dot_general(left, right, dims, preferred_element_type=jnp.float32)


def prepare_kernel(
    order_ref, doc_ref, q_first, q_second, g_first, g_second, q_rows, g_rows, facts
):
    slabs = order_ref.shape[0]
    own = q_rows.shape[0]
    slab = q_first.shape[0] // own
    heads = q_first.shape[1] // HD
    first_slab = lax.axis_index("ctx") * own
    for i in range(slabs, FACTS):
        facts[i] = 0

    def invert(i, carried):
        facts[order_ref[i]] = i
        return carried

    lax.fori_loop(0, slabs, invert, 0)
    docs = doc_ref[...]
    for i in range(3):
        facts[FACTS + i] = jnp.sum((docs <= i).astype(jnp.int32))
    for mine in range(own):
        facts[FACTS + 3 + mine] = order_ref[first_slab + mine]
        rows = slice(mine * slab, (mine + 1) * slab)
        for layer, (q_ref, g_ref) in enumerate(((q_first, g_first), (q_second, g_second))):
            for head in range(heads):
                at = (layer * heads + head) * slab
                cols = slice(head * HD, (head + 1) * HD)
                q_rows[mine, at : at + slab, :] = q_ref[rows, cols]
                g_rows[mine, at : at + slab, :] = g_ref[rows, cols]


def key_range(facts, mine, slab):
    pos0 = facts[FACTS + 3 + mine] * slab
    low = jnp.int32(0)
    for i in range(3):
        low = jnp.where(pos0 >= facts[FACTS + i], facts[FACTS + i], low)
    low = low // slab
    return pos0, low, pos0 + slab - low * slab


def for_size(need, work):
    for i, size in enumerate(SIZES):
        fits = need <= size
        if i:
            fits = fits & (need > SIZES[i - 1])
        pl.when(fits)(functools.partial(work, size))


def places(facts, low, start, size, slab):
    first = low + start // slab
    return [
        pl.ds(pl.multiple_of(facts[first + j] * slab, slab), slab) for j in range(size // slab)
    ]


def chunks(size):
    return [(start, min(CHUNK, size - start)) for start in range(0, size, CHUNK)]


def main_kernel(
    slab, facts, kv_ref, q_rows, g_rows, ds_ref, kvg_ref, scores_ref, grads_ref, key_sum
):
    own, width, _ = q_rows.shape
    scale = 1.0 / math.sqrt(HD)
    scale2 = scale * math.log2(math.e)
    key_sum[...] = jnp.zeros_like(key_sum)

    def one_slab(mine, carried):
        pos0, low, need = key_range(facts, mine, slab)
        row_pos = pos0 + (lax.broadcasted_iota(jnp.int32, (1, HD), 1) & (slab - 1))
        row_doc = jnp.zeros((1, HD), jnp.int32)
        for i in range(3):
            row_doc = jnp.where(row_pos >= facts[FACTS + i], facts[FACTS + i], row_doc)

        def work(size):
            q, g = q_rows[mine], g_rows[mine]
            top = jnp.full((1, width), MASKED_SCORE, jnp.float32)
            norm = weighted = jnp.zeros((1, width), jnp.float32)
            for start, part in chunks(size):
                key_pos = low * slab + start + lax.broadcasted_iota(jnp.int32, (part, HD), 0)
                allowed = (key_pos <= row_pos) & (key_pos >= row_doc)
                allowed = jnp.concatenate([allowed] * (width // HD), axis=1)
                at = places(facts, low, start, part, slab)
                rows = slice(start, start + part)
                keys = jnp.concatenate([kv_ref[a, :HD] for a in at], axis=0)
                values = jnp.concatenate([kv_ref[a, HD:] for a in at], axis=0)
                s = jnp.where(allowed, dot(keys, q, NT) * scale2, MASKED_SCORE)
                scores_ref[rows, :] = s
                dp = dot(values, g, NT)
                grads_ref[rows, :] = dp
                new_top = jnp.maximum(top, jnp.max(s, axis=0, keepdims=True))
                e = jnp.exp2(s - new_top)
                fix = jnp.exp2(top - new_top)
                norm = norm * fix + jnp.sum(e, axis=0, keepdims=True)
                weighted = weighted * fix + jnp.sum(e * dp, axis=0, keepdims=True)
                top = new_top
            lse = top + jnp.log2(norm)
            delta = weighted / norm
            for start, part in chunks(size):
                at = places(facts, low, start, part, slab)
                rows = slice(start, start + part)
                p = jnp.exp2(scores_ref[rows, :] - lse)
                ds = (p * (grads_ref[rows, :] - delta)).astype(jnp.bfloat16)
                ds_ref[mine, rows, :] = ds
                dv = dot(p.astype(jnp.bfloat16), g, NN)
                dk = dot(ds, q, NN)
                for j, a in enumerate(at):
                    piece = slice(j * slab, (j + 1) * slab)
                    key_sum[a, :HD] += dk[piece] * scale
                    key_sum[a, HD:] += dv[piece]

        for_size(need, work)
        return carried

    lax.fori_loop(0, own, one_slab, 0)
    kvg_ref[...] = key_sum[...].astype(jnp.bfloat16)


def query_kernel(facts, kv_ref, ds_ref, dq_first, dq_second):
    own = ds_ref.shape[0]
    slab = dq_first.shape[0] // own
    heads = dq_first.shape[1] // HD
    scale = 1.0 / math.sqrt(HD)

    def one_slab(mine, carried):
        _, low, need = key_range(facts, mine, slab)
        rows = pl.ds(pl.multiple_of(mine * slab, slab), slab)

        def work(size):
            at = places(facts, low, 0, size, slab)
            keys = jnp.concatenate([kv_ref[a, :HD] for a in at], axis=0)
            dq = dot(keys.T, ds_ref[mine, :size, :], NN) * scale
            dq = dq.T.astype(jnp.bfloat16)
            for layer, out in enumerate((dq_first, dq_second)):
                for head in range(heads):
                    at = (layer * heads + head) * slab
                    out[rows, head * HD : (head + 1) * HD] = dq[at : at + slab, :]

        for_size(need, work)
        return carried

    lax.fori_loop(0, own, one_slab, 0)


def cost(flops, size):
    return pl.CostEstimate(flops=flops, bytes_accessed=size, transcendentals=0)


VMEM = pl.BlockSpec(memory_space=pltpu.VMEM)
SMEM = pl.BlockSpec(memory_space=pltpu.SMEM)
ROOM = pltpu.CompilerParams(vmem_limit_bytes=40 * 1024 * 1024)


def prepare(slab_order, doc_ids, q_first, q_second, g_first, g_second, own):
    rows, width = q_first.shape
    stacked = jax.ShapeDtypeStruct((own, 2 * rows * (width // HD) // own, HD), jnp.bfloat16)
    return pl.pallas_call(
        prepare_kernel,
        out_shape=(stacked, stacked, jax.ShapeDtypeStruct((FACTS + 8,), jnp.int32)),
        in_specs=[SMEM] + [VMEM] * 5,
        out_specs=(VMEM, VMEM, SMEM),
        cost_estimate=cost(0, 16 * rows * width),
    )(slab_order, doc_ids.reshape(-1, HD), q_first, q_second, g_first, g_second)


def key_terms(facts, kv, q_rows, g_rows, slab):
    own, cols, _ = q_rows.shape
    most = SIZES[-1]
    return pl.pallas_call(
        functools.partial(main_kernel, slab),
        out_shape=(
            jax.ShapeDtypeStruct((own, most, cols), jnp.bfloat16),
            jax.ShapeDtypeStruct(kv.shape, jnp.bfloat16),
        ),
        in_specs=[SMEM] + [VMEM] * 3,
        out_specs=(VMEM,) * 2,
        scratch_shapes=[
            pltpu.VMEM((most, cols), jnp.float32),
            pltpu.VMEM((most, cols), jnp.float32),
            pltpu.VMEM(kv.shape, jnp.float32),
        ],
        compiler_params=ROOM,
        cost_estimate=cost(8 * own * most * cols * HD, 4 * own * most * cols),
    )(facts, kv, q_rows, g_rows)


def query_grads(facts, kv, ds, rows, width):
    out = jax.ShapeDtypeStruct((rows, width), jnp.bfloat16)
    return pl.pallas_call(
        query_kernel,
        out_shape=(out, out),
        in_specs=[SMEM] + [VMEM] * 2,
        out_specs=(VMEM,) * 2,
        compiler_params=ROOM,
        cost_estimate=cost(2 * ds.size * HD, 2 * ds.size),
    )(facts, kv, ds)


SIDE = 4
ALONG_X = [[x * SIDE + y for x in range(SIDE)] for y in range(SIDE)]
ALONG_Y = [[x * SIDE + y for y in range(SIDE)] for x in range(SIDE)]


def exchange(blocks, groups):
    return lax.all_to_all(blocks, "ctx", 0, 0, axis_index_groups=groups)


def spread(block, groups):
    copies = jnp.broadcast_to(block[None], (SIDE,) + block.shape)
    return exchange(copies, groups).reshape(SIDE * block.shape[0], block.shape[1])


def per_device(
    slab_order,
    doc_ids,
    query_first,
    query_second,
    shared_keys,
    shared_values,
    out_grad_first,
    out_grad_second,
):
    rows, width = query_first.shape
    slab = rows * lax.axis_size("ctx") // slab_order.shape[0]
    own = rows // slab
    kv = jnp.concatenate([shared_keys, shared_values], axis=1)
    kv = spread(spread(kv, ALONG_Y), ALONG_X)
    q_rows, g_rows, facts = prepare(
        slab_order, doc_ids, query_first, query_second, out_grad_first, out_grad_second, own
    )
    ds, terms = key_terms(facts, kv, q_rows, g_rows, slab)
    dq_first, dq_second = query_grads(facts, kv, ds, rows, width)
    parts = exchange(terms.reshape(SIDE, -1, 2 * HD), ALONG_X)
    summed = jnp.sum(parts.astype(jnp.float32), axis=0).astype(jnp.bfloat16)
    parts = exchange(summed.reshape(SIDE, -1, 2 * HD), ALONG_Y)
    dk = jnp.sum(parts[:, :, :HD].astype(jnp.float32), axis=0).astype(jnp.bfloat16)
    dv = jnp.sum(parts[:, :, HD:].astype(jnp.float32), axis=0).astype(jnp.bfloat16)
    return (dq_first, dq_second, dk, dv)


def solution(mesh):
    rows = P(("dp", "ctx"), "head")
    return jax.shard_map(
        per_device,
        mesh=mesh,
        in_specs=(P("dp"), P("dp")) + (rows,) * 6,
        out_specs=(rows,) * 4,
        check_vma=False,
    )
```

```python
import functools
import math

import jax
import jax.numpy as jnp
from jax import lax
from jax.experimental import pallas as pl
from jax.experimental.pallas import tpu as pltpu
from jax.sharding import PartitionSpec as P

HD = 128
SIZES = (256, 512, 768, 1024, 1152)
CHUNK = 512
PLACES = 56
MASKED_SCORE = -1e30
NT = (((1,), (1,)), ((), ()))
NN = (((1,), (0,)), ((), ()))


def dot(left, right, dims):
    return lax.dot_general(left, right, dims, preferred_element_type=jnp.float32)


def for_size(need, work):
    for i, size in enumerate(SIZES):
        fits = need <= size
        if i:
            fits = fits & (need > SIZES[i - 1])
        pl.when(fits)(functools.partial(work, size))


def places(facts, low, start, size, slab):
    first = low + start // slab
    return [
        pl.ds(pl.multiple_of(facts[first + j] * slab, slab), slab) for j in range(size // slab)
    ]


def chunks(size):
    return [(start, min(CHUNK, size - start)) for start in range(0, size, CHUNK)]


def attention_kernel(
    order_hbm,
    doc_ref,
    q_first,
    q_second,
    g_first,
    g_second,
    kv_ref,
    dq_first,
    dq_second,
    kvg_ref,
    order_ref,
    facts,
    q_rows,
    g_rows,
    scores_ref,
    grads_ref,
    ds_ref,
    key_sum,
    order_sem,
):
    slabs = order_ref.shape[0]
    own, width, _ = q_rows.shape
    slab = q_first.shape[0] // own
    heads = q_first.shape[1] // HD
    scale = 1.0 / math.sqrt(HD)
    scale2 = scale * math.log2(math.e)
    order_copy = pltpu.make_async_copy(order_hbm, order_ref, order_sem)
    order_copy.start()

    key_sum[...] = jnp.zeros_like(key_sum)
    for mine in range(own):
        rows = slice(mine * slab, (mine + 1) * slab)
        for layer, (q_ref, g_ref) in enumerate(((q_first, g_first), (q_second, g_second))):
            for head in range(heads):
                at = (layer * heads + head) * slab
                cols = slice(head * HD, (head + 1) * HD)
                q_rows[mine, at : at + slab, :] = q_ref[rows, cols]
                g_rows[mine, at : at + slab, :] = g_ref[rows, cols]
    docs = doc_ref[...]
    bounds = [jnp.sum((docs <= i).astype(jnp.int32)) for i in range(3)]

    order_copy.wait()
    for i in range(slabs, PLACES):
        facts[i] = 0

    def invert(i, carried):
        facts[order_ref[i]] = i
        return carried

    lax.fori_loop(0, slabs, invert, 0)
    first_slab = lax.axis_index("ctx") * own

    def one_slab(mine, carried):
        pos0 = order_ref[first_slab + mine] * slab
        row_pos = pos0 + (lax.broadcasted_iota(jnp.int32, (1, HD), 1) & (slab - 1))
        row_doc = jnp.zeros((1, HD), jnp.int32)
        low = jnp.int32(0)
        for bound in bounds:
            row_doc = jnp.where(row_pos >= bound, bound, row_doc)
            low = jnp.where(pos0 >= bound, bound, low)
        low = low // slab
        out_rows = pl.ds(pl.multiple_of(mine * slab, slab), slab)

        def work(size):
            q, g = q_rows[mine], g_rows[mine]
            top = jnp.full((1, width), MASKED_SCORE, jnp.float32)
            norm = weighted = jnp.zeros((1, width), jnp.float32)
            for start, part in chunks(size):
                key_pos = low * slab + start + lax.broadcasted_iota(jnp.int32, (part, HD), 0)
                allowed = (key_pos <= row_pos) & (key_pos >= row_doc)
                allowed = jnp.concatenate([allowed] * (width // HD), axis=1)
                at = places(facts, low, start, part, slab)
                rows = slice(start, start + part)
                keys = jnp.concatenate([kv_ref[a, :HD] for a in at], axis=0)
                values = jnp.concatenate([kv_ref[a, HD:] for a in at], axis=0)
                s = jnp.where(allowed, dot(keys, q, NT) * scale2, MASKED_SCORE)
                scores_ref[rows, :] = s
                dp = dot(values, g, NT)
                grads_ref[rows, :] = dp
                new_top = jnp.maximum(top, jnp.max(s, axis=0, keepdims=True))
                e = jnp.exp2(s - new_top)
                fix = jnp.exp2(top - new_top)
                norm = norm * fix + jnp.sum(e, axis=0, keepdims=True)
                weighted = weighted * fix + jnp.sum(e * dp, axis=0, keepdims=True)
                top = new_top
            lse = top + jnp.log2(norm)
            delta = weighted / norm
            for start, part in chunks(size):
                at = places(facts, low, start, part, slab)
                rows = slice(start, start + part)
                p = jnp.exp2(scores_ref[rows, :] - lse)
                ds = (p * (grads_ref[rows, :] - delta)).astype(jnp.bfloat16)
                ds_ref[rows, :] = ds
                dv = dot(p.astype(jnp.bfloat16), g, NN)
                dk = dot(ds, q, NN)
                for j, a in enumerate(at):
                    piece = slice(j * slab, (j + 1) * slab)
                    key_sum[a, :HD] += dk[piece] * scale
                    key_sum[a, HD:] += dv[piece]
            at = places(facts, low, 0, size, slab)
            keys = jnp.concatenate([kv_ref[a, :HD] for a in at], axis=0)
            dq = (dot(keys.T, ds_ref[:size, :], NN) * scale).T.astype(jnp.bfloat16)
            for layer, out in enumerate((dq_first, dq_second)):
                for head in range(heads):
                    at = (layer * heads + head) * slab
                    out[out_rows, head * HD : (head + 1) * HD] = dq[at : at + slab, :]

        for_size(pos0 + slab - low * slab, work)
        return carried

    lax.fori_loop(0, own, one_slab, 0)
    kvg_ref[...] = key_sum[...].astype(jnp.bfloat16)


def attention(slab_order, doc_ids, q_first, q_second, g_first, g_second, kv):
    rows, width = q_first.shape
    slab = kv.shape[0] // slab_order.shape[0]
    own = rows // slab
    cols = 2 * (width // HD) * slab
    most = SIZES[-1]
    out = jax.ShapeDtypeStruct((rows, width), jnp.bfloat16)
    vmem = pl.BlockSpec(memory_space=pltpu.VMEM)
    return pl.pallas_call(
        attention_kernel,
        out_shape=(out, out, jax.ShapeDtypeStruct(kv.shape, jnp.bfloat16)),
        in_specs=[pl.BlockSpec(memory_space=pltpu.HBM)] + [vmem] * 6,
        out_specs=(vmem,) * 3,
        scratch_shapes=[
            pltpu.SMEM(slab_order.shape, jnp.int32),
            pltpu.SMEM((PLACES,), jnp.int32),
            pltpu.VMEM((own, cols, HD), jnp.bfloat16),
            pltpu.VMEM((own, cols, HD), jnp.bfloat16),
            pltpu.VMEM((most, cols), jnp.float32),
            pltpu.VMEM((most, cols), jnp.float32),
            pltpu.VMEM((most, cols), jnp.bfloat16),
            pltpu.VMEM(kv.shape, jnp.float32),
            pltpu.SemaphoreType.DMA(()),
        ],
        compiler_params=pltpu.CompilerParams(vmem_limit_bytes=32 * 1024 * 1024),
    )(slab_order, doc_ids.reshape(-1, HD), q_first, q_second, g_first, g_second, kv)


SIDE = 4
ALONG_X = [[x * SIDE + y for x in range(SIDE)] for y in range(SIDE)]
ALONG_Y = [[x * SIDE + y for y in range(SIDE)] for x in range(SIDE)]


def exchange(blocks, groups):
    return lax.all_to_all(blocks, "ctx", 0, 0, axis_index_groups=groups)


def spread(block, groups):
    copies = jnp.broadcast_to(block[None], (SIDE,) + block.shape)
    return exchange(copies, groups).reshape(SIDE * block.shape[0], block.shape[1])


def per_device(
    slab_order,
    doc_ids,
    query_first,
    query_second,
    shared_keys,
    shared_values,
    out_grad_first,
    out_grad_second,
):
    kv = jnp.concatenate([shared_keys, shared_values], axis=1)
    kv = spread(spread(kv, ALONG_Y), ALONG_X)
    dq_first, dq_second, terms = attention(
        slab_order, doc_ids, query_first, query_second, out_grad_first, out_grad_second, kv
    )
    parts = exchange(terms.reshape(SIDE, -1, 2 * HD), ALONG_X)
    summed = jnp.sum(parts.astype(jnp.float32), axis=0).astype(jnp.bfloat16)
    parts = exchange(summed.reshape(SIDE, -1, 2 * HD), ALONG_Y)
    dk = jnp.sum(parts[:, :, :HD].astype(jnp.float32), axis=0).astype(jnp.bfloat16)
    dv = jnp.sum(parts[:, :, HD:].astype(jnp.float32), axis=0).astype(jnp.bfloat16)
    return (dq_first, dq_second, dk, dv)


def solution(mesh):
    rows = P(("dp", "ctx"), "head")
    return jax.shard_map(
        per_device,
        mesh=mesh,
        in_specs=(P("dp"), P("dp")) + (rows,) * 6,
        out_specs=(rows,) * 4,
        check_vma=False,
    )
```

```python
import functools
import math

import jax
import jax.numpy as jnp
from jax import lax
from jax.experimental import pallas as pl
from jax.experimental.pallas import tpu as pltpu
from jax.sharding import PartitionSpec as P

HD = 128
SIZES = (256, 512, 768, 1024, 1152)
CHUNK = 512
FACTS = 48
MASKED_SCORE = -1e30
NT = (((1,), (1,)), ((), ()))
NN = (((1,), (0,)), ((), ()))


def dot(left, right, dims):
    return lax.dot_general(left, right, dims, preferred_element_type=jnp.float32)


def prepare_kernel(
    order_ref, doc_ref, q_first, q_second, g_first, g_second, q_rows, g_rows, facts
):
    slabs = order_ref.shape[0]
    own = q_rows.shape[0]
    slab = q_first.shape[0] // own
    heads = q_first.shape[1] // HD
    first_slab = lax.axis_index("ctx") * own
    for i in range(slabs, FACTS):
        facts[i] = 0

    def invert(i, carried):
        facts[order_ref[i]] = i
        return carried

    lax.fori_loop(0, slabs, invert, 0)
    docs = doc_ref[...]
    for i in range(3):
        facts[FACTS + i] = jnp.sum((docs <= i).astype(jnp.int32))
    for mine in range(own):
        facts[FACTS + 3 + mine] = order_ref[first_slab + mine]
        rows = slice(mine * slab, (mine + 1) * slab)
        for layer, (q_ref, g_ref) in enumerate(((q_first, g_first), (q_second, g_second))):
            for head in range(heads):
                at = (layer * heads + head) * slab
                cols = slice(head * HD, (head + 1) * HD)
                q_rows[mine, at : at + slab, :] = q_ref[rows, cols]
                g_rows[mine, at : at + slab, :] = g_ref[rows, cols]


def key_range(facts, mine, slab):
    pos0 = facts[FACTS + 3 + mine] * slab
    low = jnp.int32(0)
    for i in range(3):
        low = jnp.where(pos0 >= facts[FACTS + i], facts[FACTS + i], low)
    low = low // slab
    return pos0, low, pos0 + slab - low * slab


def for_size(need, work):
    for i, size in enumerate(SIZES):
        fits = need <= size
        if i:
            fits = fits & (need > SIZES[i - 1])
        pl.when(fits)(functools.partial(work, size))


def places(facts, low, start, size, slab):
    first = low + start // slab
    return [
        pl.ds(pl.multiple_of(facts[first + j] * slab, slab), slab) for j in range(size // slab)
    ]


def chunks(size):
    return [(start, min(CHUNK, size - start)) for start in range(0, size, CHUNK)]


def score_blocks(facts, mine, slab, size, kv_ref, q, g):
    pos0, low, _ = key_range(facts, mine, slab)
    row_pos = pos0 + (lax.broadcasted_iota(jnp.int32, (1, HD), 1) & (slab - 1))
    row_doc = jnp.zeros((1, HD), jnp.int32)
    for i in range(3):
        row_doc = jnp.where(row_pos >= facts[FACTS + i], facts[FACTS + i], row_doc)
    scale2 = math.log2(math.e) / math.sqrt(HD)
    for start, part in chunks(size):
        key_pos = low * slab + start + lax.broadcasted_iota(jnp.int32, (part, HD), 0)
        allowed = (key_pos <= row_pos) & (key_pos >= row_doc)
        allowed = jnp.concatenate([allowed] * (q.shape[0] // HD), axis=1)
        at = places(facts, low, start, part, slab)
        keys = jnp.concatenate([kv_ref[a, :HD] for a in at], axis=0)
        values = jnp.concatenate([kv_ref[a, HD:] for a in at], axis=0)
        s = jnp.where(allowed, dot(keys, q, NT) * scale2, MASKED_SCORE)
        yield slice(start, start + part), at, keys, s, dot(values, g, NT)


def main_kernel(
    slab, facts, kv_ref, q_rows, g_rows, stats, kvg_ref, scores_ref, grads_ref, key_sum
):
    own, width, _ = q_rows.shape
    scale = 1.0 / math.sqrt(HD)
    key_sum[...] = jnp.zeros_like(key_sum)

    def one_slab(mine, carried):
        def work(size):
            q, g = q_rows[mine], g_rows[mine]
            top = jnp.full((1, width), MASKED_SCORE, jnp.float32)
            norm = weighted = jnp.zeros((1, width), jnp.float32)
            blocks = []
            for rows, at, _, s, dp in score_blocks(facts, mine, slab, size, kv_ref, q, g):
                blocks.append((rows, at))
                scores_ref[rows, :] = s
                grads_ref[rows, :] = dp
                new_top = jnp.maximum(top, jnp.max(s, axis=0, keepdims=True))
                e = jnp.exp2(s - new_top)
                fix = jnp.exp2(top - new_top)
                norm = norm * fix + jnp.sum(e, axis=0, keepdims=True)
                weighted = weighted * fix + jnp.sum(e * dp, axis=0, keepdims=True)
                top = new_top
            lse = top + jnp.log2(norm)
            delta = weighted / norm
            stats[mine, 0:1, :] = lse
            stats[mine, 1:2, :] = delta
            for rows, at in blocks:
                p = jnp.exp2(scores_ref[rows, :] - lse)
                ds = (p * (grads_ref[rows, :] - delta)).astype(jnp.bfloat16)
                dv = dot(p.astype(jnp.bfloat16), g, NN)
                dk = dot(ds, q, NN)
                for j, a in enumerate(at):
                    piece = slice(j * slab, (j + 1) * slab)
                    key_sum[a, :HD] += dk[piece] * scale
                    key_sum[a, HD:] += dv[piece]

        for_size(key_range(facts, mine, slab)[2], work)
        return carried

    lax.fori_loop(0, own, one_slab, 0)
    kvg_ref[...] = key_sum[...].astype(jnp.bfloat16)


def query_kernel(facts, kv_ref, q_rows, g_rows, stats, dq_first, dq_second):
    own, width, _ = q_rows.shape
    slab = dq_first.shape[0] // own
    heads = dq_first.shape[1] // HD
    scale = 1.0 / math.sqrt(HD)

    def one_slab(mine, carried):
        out_rows = pl.ds(pl.multiple_of(mine * slab, slab), slab)

        def work(size):
            lse, delta = stats[mine, 0:1, :], stats[mine, 1:2, :]
            dq = jnp.zeros((HD, width), jnp.float32)
            for _, _, keys, s, dp in score_blocks(
                facts, mine, slab, size, kv_ref, q_rows[mine], g_rows[mine]
            ):
                ds = (jnp.exp2(s - lse) * (dp - delta)).astype(jnp.bfloat16)
                dq = dq + dot(keys.T, ds, NN)
            dq = (dq * scale).T.astype(jnp.bfloat16)
            for layer, out in enumerate((dq_first, dq_second)):
                for head in range(heads):
                    at = (layer * heads + head) * slab
                    out[out_rows, head * HD : (head + 1) * HD] = dq[at : at + slab, :]

        for_size(key_range(facts, mine, slab)[2], work)
        return carried

    lax.fori_loop(0, own, one_slab, 0)


def cost(flops, size):
    return pl.CostEstimate(flops=flops, bytes_accessed=size, transcendentals=0)


def room(mib):
    return pltpu.CompilerParams(vmem_limit_bytes=mib * 1024 * 1024)


VMEM = pl.BlockSpec(memory_space=pltpu.VMEM)
SMEM = pl.BlockSpec(memory_space=pltpu.SMEM)


def prepare(slab_order, doc_ids, q_first, q_second, g_first, g_second, own):
    rows, width = q_first.shape
    stacked = jax.ShapeDtypeStruct((own, 2 * rows * (width // HD) // own, HD), jnp.bfloat16)
    return pl.pallas_call(
        prepare_kernel,
        out_shape=(stacked, stacked, jax.ShapeDtypeStruct((FACTS + 8,), jnp.int32)),
        in_specs=[SMEM] + [VMEM] * 5,
        out_specs=(VMEM, VMEM, SMEM),
        compiler_params=room(4),
        cost_estimate=cost(0, 16 * rows * width),
    )(slab_order, doc_ids.reshape(-1, HD), q_first, q_second, g_first, g_second)


def key_terms(facts, kv, q_rows, g_rows, slab):
    own, cols, _ = q_rows.shape
    most = SIZES[-1]
    return pl.pallas_call(
        functools.partial(main_kernel, slab),
        out_shape=(
            jax.ShapeDtypeStruct((own, 8, cols), jnp.float32),
            jax.ShapeDtypeStruct(kv.shape, jnp.bfloat16),
        ),
        in_specs=[SMEM] + [VMEM] * 3,
        out_specs=(VMEM,) * 2,
        scratch_shapes=[
            pltpu.VMEM((most, cols), jnp.float32),
            pltpu.VMEM((most, cols), jnp.float32),
            pltpu.VMEM(kv.shape, jnp.float32),
        ],
        compiler_params=room(24),
        cost_estimate=cost(8 * own * most * cols * HD, 4 * kv.size),
    )(facts, kv, q_rows, g_rows)


def query_grads(facts, kv, q_rows, g_rows, stats, rows, width):
    own, cols, _ = q_rows.shape
    out = jax.ShapeDtypeStruct((rows, width), jnp.bfloat16)
    return pl.pallas_call(
        query_kernel,
        out_shape=(out, out),
        in_specs=[SMEM] + [VMEM] * 4,
        out_specs=(VMEM,) * 2,
        compiler_params=room(20),
        cost_estimate=cost(6 * own * SIZES[-1] * cols * HD, 4 * kv.size),
    )(facts, kv, q_rows, g_rows, stats)


SIDE = 4
ALONG_X = [[x * SIDE + y for x in range(SIDE)] for y in range(SIDE)]
ALONG_Y = [[x * SIDE + y for y in range(SIDE)] for x in range(SIDE)]


def exchange(blocks, groups):
    return lax.all_to_all(blocks, "ctx", 0, 0, axis_index_groups=groups)


def spread(block, groups):
    copies = jnp.broadcast_to(block[None], (SIDE,) + block.shape)
    return exchange(copies, groups).reshape(SIDE * block.shape[0], block.shape[1])


def per_device(
    slab_order,
    doc_ids,
    query_first,
    query_second,
    shared_keys,
    shared_values,
    out_grad_first,
    out_grad_second,
):
    rows, width = query_first.shape
    slab = rows * lax.axis_size("ctx") // slab_order.shape[0]
    own = rows // slab
    kv = jnp.concatenate([shared_keys, shared_values], axis=1)
    kv = spread(kv, ALONG_Y)
    ready = prepare(
        slab_order, doc_ids, query_first, query_second, out_grad_first, out_grad_second, own
    )
    kv, q_rows, g_rows, facts = lax.optimization_barrier((kv, *ready))
    kv = spread(kv, ALONG_X)
    stats, terms = key_terms(facts, kv, q_rows, g_rows, slab)
    dq_first, dq_second = query_grads(facts, kv, q_rows, g_rows, stats, rows, width)
    parts = exchange(terms.reshape(SIDE, -1, 2 * HD), ALONG_X)
    summed = jnp.sum(parts.astype(jnp.float32), axis=0).astype(jnp.bfloat16)
    parts = exchange(summed.reshape(SIDE, -1, 2 * HD), ALONG_Y)
    dk = jnp.sum(parts[:, :, :HD].astype(jnp.float32), axis=0).astype(jnp.bfloat16)
    dv = jnp.sum(parts[:, :, HD:].astype(jnp.float32), axis=0).astype(jnp.bfloat16)
    return (dq_first, dq_second, dk, dv)


def solution(mesh):
    rows = P(("dp", "ctx"), "head")
    return jax.shard_map(
        per_device,
        mesh=mesh,
        in_specs=(P("dp"), P("dp")) + (rows,) * 6,
        out_specs=(rows,) * 4,
        check_vma=False,
    )
```

```python
import functools
import math

import jax
import jax.numpy as jnp
from jax import lax
from jax.experimental import pallas as pl
from jax.experimental.pallas import tpu as pltpu
from jax.sharding import PartitionSpec as P

HD = 128
SIZES = (128, 256, 384, 512, 640, 768, 896, 1024, 1152)
CHUNK = 512
PLACES = 56
MASKED_SCORE = -1e30
NT = (((1,), (1,)), ((), ()))
NN = (((1,), (0,)), ((), ()))


def dot(left, right, dims):
    return lax.dot_general(left, right, dims, preferred_element_type=jnp.float32)


def for_size(need, work):
    for i, size in enumerate(SIZES):
        fits = need <= size
        if i:
            fits = fits & (need > SIZES[i - 1])
        pl.when(fits)(functools.partial(work, size))


def places(facts, low, start, size, slab):
    first = low + start // slab
    return [
        pl.ds(pl.multiple_of(facts[first + j] * slab, slab), slab) for j in range(size // slab)
    ]


def chunks(size):
    return [(start, min(CHUNK, size - start)) for start in range(0, size, CHUNK)]


def attention_kernel(
    order_hbm,
    doc_ref,
    q_first,
    q_second,
    g_first,
    g_second,
    kv_ref,
    dq_first,
    dq_second,
    kvg_ref,
    order_ref,
    facts,
    q_rows,
    g_rows,
    scores_ref,
    grads_ref,
    ds_ref,
    key_sum,
    dq_stage,
    order_sem,
    dq_sems,
):
    slabs = order_ref.shape[0]
    own, width, _ = q_rows.shape
    slab = q_first.shape[0] // own
    heads = q_first.shape[1] // HD
    scale = 1.0 / math.sqrt(HD)
    scale2 = scale * math.log2(math.e)
    order_copy = pltpu.make_async_copy(order_hbm, order_ref, order_sem)
    order_copy.start()

    key_sum[...] = jnp.zeros_like(key_sum)
    docs = doc_ref[...]
    bounds = [jnp.sum((docs <= i).astype(jnp.int32)) for i in range(3)]
    for mine in range(own):
        rows = slice(mine * slab, (mine + 1) * slab)
        for layer, (q_ref, g_ref) in enumerate(((q_first, g_first), (q_second, g_second))):
            for head in range(heads):
                at = (layer * heads + head) * slab
                cols = slice(head * HD, (head + 1) * HD)
                q_rows[mine, at : at + slab, :] = q_ref[rows, cols]
                g_rows[mine, at : at + slab, :] = g_ref[rows, cols]
    order_copy.wait()
    for i in range(slabs, PLACES):
        facts[i] = 0
    for i in range(slabs):
        facts[order_ref[i]] = i
    first_slab = lax.axis_index("ctx") * own

    def dq_copies(mine):
        rows = pl.ds(pl.multiple_of(mine * slab, slab), slab)
        return [
            pltpu.make_async_copy(dq_stage.at[layer, rows], out.at[rows], dq_sems.at[mine, layer])
            for layer, out in enumerate((dq_first, dq_second))
        ]

    def one_slab(mine, carried):
        pos0 = order_ref[first_slab + mine] * slab
        row_pos = pos0 + (lax.broadcasted_iota(jnp.int32, (1, HD), 1) & (slab - 1))
        row_doc = jnp.zeros((1, HD), jnp.int32)
        low = jnp.int32(0)
        for bound in bounds:
            row_doc = jnp.where(row_pos >= bound, bound, row_doc)
            low = jnp.where(pos0 >= bound, bound, low)
        low = low // slab
        out_rows = pl.ds(pl.multiple_of(mine * slab, slab), slab)

        def work(size):
            q, g = q_rows[mine], g_rows[mine]
            top = jnp.full((1, width), MASKED_SCORE, jnp.float32)
            norm = weighted = jnp.zeros((1, width), jnp.float32)
            for start, part in chunks(size):
                key_pos = low * slab + start + lax.broadcasted_iota(jnp.int32, (part, HD), 0)
                allowed = (key_pos <= row_pos) & (key_pos >= row_doc)
                allowed = jnp.concatenate([allowed] * (width // HD), axis=1)
                at = places(facts, low, start, part, slab)
                rows = slice(start, start + part)
                keys = jnp.concatenate([kv_ref[a, :HD] for a in at], axis=0)
                values = jnp.concatenate([kv_ref[a, HD:] for a in at], axis=0)
                s = jnp.where(allowed, dot(keys, q, NT) * scale2, MASKED_SCORE)
                scores_ref[rows, :] = s
                dp = dot(values, g, NT)
                grads_ref[rows, :] = dp
                new_top = jnp.maximum(top, jnp.max(s, axis=0, keepdims=True))
                e = jnp.exp2(s - new_top)
                fix = jnp.exp2(top - new_top)
                norm = norm * fix + jnp.sum(e, axis=0, keepdims=True)
                weighted = weighted * fix + jnp.sum(e * dp, axis=0, keepdims=True)
                top = new_top
            lse = top + jnp.log2(norm)
            delta = weighted / norm
            for start, part in chunks(size):
                at = places(facts, low, start, part, slab)
                rows = slice(start, start + part)
                p = jnp.exp2(scores_ref[rows, :] - lse)
                ds = (p * (grads_ref[rows, :] - delta)).astype(jnp.bfloat16)
                ds_ref[rows, :] = ds
                dv = dot(p.astype(jnp.bfloat16), g, NN)
                dk = dot(ds, q, NN)
                for j, a in enumerate(at):
                    piece = slice(j * slab, (j + 1) * slab)
                    key_sum[a, :HD] += dk[piece] * scale
                    key_sum[a, HD:] += dv[piece]
            at = places(facts, low, 0, size, slab)
            keys = jnp.concatenate([kv_ref[a, :HD] for a in at], axis=0)
            dq = (dot(keys.T, ds_ref[:size, :], NN) * scale).T.astype(jnp.bfloat16)
            for layer in range(2):
                for head in range(heads):
                    at = (layer * heads + head) * slab
                    cols = slice(head * HD, (head + 1) * HD)
                    dq_stage[layer, out_rows, cols] = dq[at : at + slab, :]

        for_size(pos0 + slab - low * slab, work)
        for copy in dq_copies(mine):
            copy.start()
        return carried

    lax.fori_loop(0, own, one_slab, 0)
    kvg_ref[...] = key_sum[...].astype(jnp.bfloat16)
    for mine in range(own):
        for copy in dq_copies(mine):
            copy.wait()


def attention(slab_order, doc_ids, q_first, q_second, g_first, g_second, kv):
    rows, width = q_first.shape
    slab = kv.shape[0] // slab_order.shape[0]
    own = rows // slab
    cols = 2 * (width // HD) * slab
    most = SIZES[-1]
    out = jax.ShapeDtypeStruct((rows, width), jnp.bfloat16)
    vmem = pl.BlockSpec(memory_space=pltpu.VMEM)
    hbm = pl.BlockSpec(memory_space=pltpu.HBM)
    slab_order = pltpu.with_memory_space_constraint(slab_order, pltpu.HBM)
    return pl.pallas_call(
        attention_kernel,
        out_shape=(out, out, jax.ShapeDtypeStruct(kv.shape, jnp.bfloat16)),
        in_specs=[hbm] + [vmem] * 6,
        out_specs=(hbm, hbm, vmem),
        scratch_shapes=[
            pltpu.SMEM(slab_order.shape, jnp.int32),
            pltpu.SMEM((PLACES,), jnp.int32),
            pltpu.VMEM((own, cols, HD), jnp.bfloat16),
            pltpu.VMEM((own, cols, HD), jnp.bfloat16),
            pltpu.VMEM((most, cols), jnp.float32),
            pltpu.VMEM((most, cols), jnp.float32),
            pltpu.VMEM((most, cols), jnp.bfloat16),
            pltpu.VMEM(kv.shape, jnp.float32),
            pltpu.VMEM((2, rows, width), jnp.bfloat16),
            pltpu.SemaphoreType.DMA(()),
            pltpu.SemaphoreType.DMA((own, 2)),
        ],
        compiler_params=pltpu.CompilerParams(vmem_limit_bytes=32 * 1024 * 1024),
    )(slab_order, doc_ids.reshape(-1, HD), q_first, q_second, g_first, g_second, kv)


SIDE = 4
ALONG_X = [[x * SIDE + y for x in range(SIDE)] for y in range(SIDE)]
ALONG_Y = [[x * SIDE + y for y in range(SIDE)] for x in range(SIDE)]


def exchange(blocks, groups):
    return lax.all_to_all(blocks, "ctx", 0, 0, axis_index_groups=groups)


def spread(block, groups):
    copies = jnp.broadcast_to(block[None], (SIDE,) + block.shape)
    return exchange(copies, groups).reshape(SIDE * block.shape[0], block.shape[1])


def per_device(
    slab_order,
    doc_ids,
    query_first,
    query_second,
    shared_keys,
    shared_values,
    out_grad_first,
    out_grad_second,
):
    kv = jnp.concatenate([shared_keys, shared_values], axis=1)
    kv = spread(spread(kv, ALONG_Y), ALONG_X)
    dq_first, dq_second, terms = attention(
        slab_order, doc_ids, query_first, query_second, out_grad_first, out_grad_second, kv
    )
    parts = exchange(terms.reshape(SIDE, -1, 2 * HD), ALONG_X)
    summed = jnp.sum(parts.astype(jnp.float32), axis=0).astype(jnp.bfloat16)
    parts = exchange(summed.reshape(SIDE, -1, 2 * HD), ALONG_Y)
    dk = jnp.sum(parts[:, :, :HD].astype(jnp.float32), axis=0).astype(jnp.bfloat16)
    dv = jnp.sum(parts[:, :, HD:].astype(jnp.float32), axis=0).astype(jnp.bfloat16)
    return (dq_first, dq_second, dk, dv)


def solution(mesh):
    rows = P(("dp", "ctx"), "head")
    return jax.shard_map(
        per_device,
        mesh=mesh,
        in_specs=(P("dp"), P("dp")) + (rows,) * 6,
        out_specs=(rows,) * 4,
        check_vma=False,
    )
```

```python
import functools
import math

import jax
import jax.numpy as jnp
from jax import lax
from jax.experimental import pallas as pl
from jax.experimental.pallas import tpu as pltpu
from jax.sharding import PartitionSpec as P

HD = 128
SIZES = (128, 256, 384, 512, 640, 768, 896, 1024, 1152)
CHUNK = 1152
PLACES = 56
MASKED_SCORE = -1e30
NT = (((1,), (1,)), ((), ()))
NN = (((1,), (0,)), ((), ()))


def dot(left, right, dims):
    return lax.dot_general(left, right, dims, preferred_element_type=jnp.float32)


def for_size(need, work):
    for i, size in enumerate(SIZES):
        fits = need <= size
        if i:
            fits = fits & (need > SIZES[i - 1])
        pl.when(fits)(functools.partial(work, size))


def places(facts, low, start, size, slab):
    first = low + start // slab
    return [
        pl.multiple_of(facts[first + j] * slab, slab) for j in range(size // slab)
    ]


def chunks(size):
    return [(start, min(CHUNK, size - start)) for start in range(0, size, CHUNK)]


def attention_kernel(
    order_hbm,
    doc_ref,
    q_first,
    q_second,
    g_first,
    g_second,
    kv_ref,
    dq_first,
    dq_second,
    kvg_ref,
    order_ref,
    facts,
    q_rows,
    g_rows,
    scores_ref,
    grads_ref,
    ds_ref,
    key_sum,
    dq_stage,
    order_sem,
    dq_sems,
):
    slabs = order_ref.shape[0]
    own, width, _ = q_rows.shape
    slab = q_first.shape[0] // own
    heads = q_first.shape[1] // HD
    scale = 1.0 / math.sqrt(HD)
    scale2 = scale * math.log2(math.e)
    order_copy = pltpu.make_async_copy(order_hbm, order_ref, order_sem)
    order_copy.start()

    key_sum[...] = jnp.zeros_like(key_sum)
    docs = doc_ref[...]
    bounds = [jnp.sum((docs <= i).astype(jnp.int32)) for i in range(3)]
    for mine in range(own):
        rows = slice(mine * slab, (mine + 1) * slab)
        for layer, (q_ref, g_ref) in enumerate(((q_first, g_first), (q_second, g_second))):
            for head in range(heads):
                at = (layer * heads + head) * slab
                cols = slice(head * HD, (head + 1) * HD)
                q_rows[mine, at : at + slab, :] = q_ref[rows, cols]
                g_rows[mine, at : at + slab, :] = g_ref[rows, cols]
    order_copy.wait()
    for i in range(slabs, PLACES):
        facts[i] = 0
    for i in range(slabs):
        facts[order_ref[i]] = i // own * 2 * own + i % own
    first_slab = lax.axis_index("ctx") * own

    def dq_copies(mine):
        rows = pl.ds(pl.multiple_of(mine * slab, slab), slab)
        return [
            pltpu.make_async_copy(dq_stage.at[layer, rows], out.at[rows], dq_sems.at[mine, layer])
            for layer, out in enumerate((dq_first, dq_second))
        ]

    def one_slab(mine, carried):
        pos0 = order_ref[first_slab + mine] * slab
        row_pos = pos0 + (lax.broadcasted_iota(jnp.int32, (1, HD), 1) & (slab - 1))
        row_doc = jnp.zeros((1, HD), jnp.int32)
        low = jnp.int32(0)
        for bound in bounds:
            row_doc = jnp.where(row_pos >= bound, bound, row_doc)
            low = jnp.where(pos0 >= bound, bound, low)
        low = low // slab
        out_rows = pl.ds(pl.multiple_of(mine * slab, slab), slab)

        def work(size):
            q, g = q_rows[mine], g_rows[mine]
            top = jnp.full((1, width), MASKED_SCORE, jnp.float32)
            norm = weighted = jnp.zeros((1, width), jnp.float32)
            for start, part in chunks(size):
                key_pos = low * slab + start + lax.broadcasted_iota(jnp.int32, (part, HD), 0)
                allowed = (key_pos <= row_pos) & (key_pos >= row_doc)
                allowed = jnp.concatenate([allowed] * (width // HD), axis=1)
                at = places(facts, low, start, part, slab)
                rows = slice(start, start + part)
                keys = jnp.concatenate([kv_ref[pl.ds(a, slab), :] for a in at], axis=0)
                values = jnp.concatenate(
                    [kv_ref[pl.ds(a + own * slab, slab), :] for a in at], axis=0
                )
                s = jnp.where(allowed, dot(keys, q, NT) * scale2, MASKED_SCORE)
                scores_ref[rows, :] = s
                dp = dot(values, g, NT)
                grads_ref[rows, :] = dp
                new_top = jnp.maximum(top, jnp.max(s, axis=0, keepdims=True))
                e = jnp.exp2(s - new_top)
                fix = jnp.exp2(top - new_top)
                norm = norm * fix + jnp.sum(e, axis=0, keepdims=True)
                weighted = weighted * fix + jnp.sum(e * dp, axis=0, keepdims=True)
                top = new_top
            lse = top + jnp.log2(norm)
            delta = weighted / norm
            for start, part in chunks(size):
                at = places(facts, low, start, part, slab)
                rows = slice(start, start + part)
                p = jnp.exp2(scores_ref[rows, :] - lse)
                ds = (p * (grads_ref[rows, :] - delta)).astype(jnp.bfloat16)
                ds_ref[rows, :] = ds
                dv = dot(p.astype(jnp.bfloat16), g, NN)
                dk = dot(ds, q, NN)
                for j, a in enumerate(at):
                    piece = slice(j * slab, (j + 1) * slab)
                    key_sum[pl.ds(a, slab), :] += dk[piece] * scale
                    key_sum[pl.ds(a + own * slab, slab), :] += dv[piece]
            at = places(facts, low, 0, size, slab)
            keys = jnp.concatenate([kv_ref[pl.ds(a, slab), :] for a in at], axis=0)
            dq = (dot(keys.T, ds_ref[:size, :], NN) * scale).T.astype(jnp.bfloat16)
            for layer in range(2):
                for head in range(heads):
                    at = (layer * heads + head) * slab
                    cols = slice(head * HD, (head + 1) * HD)
                    dq_stage[layer, out_rows, cols] = dq[at : at + slab, :]

        for_size(pos0 + slab - low * slab, work)
        for copy in dq_copies(mine):
            copy.start()
        return carried

    lax.fori_loop(0, own, one_slab, 0)
    kvg_ref[...] = key_sum[...].astype(jnp.bfloat16)
    for mine in range(own):
        for copy in dq_copies(mine):
            copy.wait()


def attention(slab_order, doc_ids, q_first, q_second, g_first, g_second, kv):
    rows, width = q_first.shape
    slab = kv.shape[0] // (2 * slab_order.shape[0])
    own = rows // slab
    cols = 2 * (width // HD) * slab
    most = SIZES[-1]
    out = jax.ShapeDtypeStruct((rows, width), jnp.bfloat16)
    vmem = pl.BlockSpec(memory_space=pltpu.VMEM)
    hbm = pl.BlockSpec(memory_space=pltpu.HBM)
    slab_order = pltpu.with_memory_space_constraint(slab_order, pltpu.HBM)
    return pl.pallas_call(
        attention_kernel,
        out_shape=(out, out, jax.ShapeDtypeStruct(kv.shape, jnp.bfloat16)),
        in_specs=[hbm] + [vmem] * 6,
        out_specs=(hbm, hbm, vmem),
        scratch_shapes=[
            pltpu.SMEM(slab_order.shape, jnp.int32),
            pltpu.SMEM((PLACES,), jnp.int32),
            pltpu.VMEM((own, cols, HD), jnp.bfloat16),
            pltpu.VMEM((own, cols, HD), jnp.bfloat16),
            pltpu.VMEM((most, cols), jnp.float32),
            pltpu.VMEM((most, cols), jnp.float32),
            pltpu.VMEM((most, cols), jnp.bfloat16),
            pltpu.VMEM(kv.shape, jnp.float32),
            pltpu.VMEM((2, rows, width), jnp.bfloat16),
            pltpu.SemaphoreType.DMA(()),
            pltpu.SemaphoreType.DMA((own, 2)),
        ],
        compiler_params=pltpu.CompilerParams(vmem_limit_bytes=32 * 1024 * 1024),
    )(slab_order, doc_ids.reshape(-1, HD), q_first, q_second, g_first, g_second, kv)


SIDE = 4
ALONG_X = [[x * SIDE + y for x in range(SIDE)] for y in range(SIDE)]
ALONG_Y = [[x * SIDE + y for y in range(SIDE)] for x in range(SIDE)]


def exchange(blocks, groups):
    return lax.all_to_all(blocks, "ctx", 0, 0, axis_index_groups=groups)


def spread(block, groups):
    copies = jnp.broadcast_to(block[None], (SIDE,) + block.shape)
    return exchange(copies, groups).reshape(SIDE * block.shape[0], block.shape[1])


def per_device(
    slab_order,
    doc_ids,
    query_first,
    query_second,
    shared_keys,
    shared_values,
    out_grad_first,
    out_grad_second,
):
    kv = jnp.concatenate([shared_keys, shared_values], axis=0)
    kv = spread(spread(kv, ALONG_Y), ALONG_X)
    dq_first, dq_second, terms = attention(
        slab_order, doc_ids, query_first, query_second, out_grad_first, out_grad_second, kv
    )
    rows = shared_keys.shape[0]
    parts = exchange(terms.reshape(SIDE, -1, HD), ALONG_X)
    summed = jnp.sum(parts.astype(jnp.float32), axis=0).astype(jnp.bfloat16)
    parts = exchange(summed.reshape(SIDE, -1, HD), ALONG_Y)
    dk = jnp.sum(parts[:, :rows].astype(jnp.float32), axis=0).astype(jnp.bfloat16)
    dv = jnp.sum(parts[:, rows:].astype(jnp.float32), axis=0).astype(jnp.bfloat16)
    return (dq_first, dq_second, dk, dv)


def solution(mesh):
    rows = P(("dp", "ctx"), "head")
    return jax.shard_map(
        per_device,
        mesh=mesh,
        in_specs=(P("dp"), P("dp")) + (rows,) * 6,
        out_specs=(rows,) * 4,
        check_vma=False,
    )
```

```python
import functools
import math

import jax
import jax.numpy as jnp
from jax import lax
from jax.experimental import pallas as pl
from jax.experimental.pallas import tpu as pltpu
from jax.sharding import PartitionSpec as P

HD = 128
SIZES = (128, 256, 384, 512, 640, 768, 896, 1024, 1088)
CHUNK = 1088
PLACES = 56
MASKED_SCORE = -1e30
NT = (((1,), (1,)), ((), ()))
NN = (((1,), (0,)), ((), ()))


def dot(left, right, dims):
    return lax.dot_general(left, right, dims, preferred_element_type=jnp.float32)


def for_size(need, work):
    for i, size in enumerate(SIZES):
        fits = need <= size
        if i:
            fits = fits & (need > SIZES[i - 1])
        pl.when(fits)(functools.partial(work, size))


def places(facts, low, start, size, slab):
    first = low + start // slab
    return [
        pl.multiple_of(facts[first + j] * slab, slab) for j in range(size // slab)
    ]


def chunks(size):
    return [(start, min(CHUNK, size - start)) for start in range(0, size, CHUNK)]


def attention_kernel(
    order_hbm,
    doc_ref,
    q_first,
    q_second,
    g_first,
    g_second,
    kv_ref,
    dq_first,
    dq_second,
    kvg_ref,
    order_ref,
    facts,
    q_rows,
    g_rows,
    scores_ref,
    grads_ref,
    ds_ref,
    key_sum,
    dq_stage,
    order_sem,
    dq_sems,
):
    slabs = order_ref.shape[0]
    own, width, _ = q_rows.shape
    slab = q_first.shape[0] // own
    heads = q_first.shape[1] // HD
    scale = 1.0 / math.sqrt(HD)
    scale2 = scale * math.log2(math.e)
    order_copy = pltpu.make_async_copy(order_hbm, order_ref, order_sem)
    order_copy.start()

    key_sum[...] = jnp.zeros_like(key_sum)
    docs = doc_ref[...]
    bounds = [jnp.sum((docs <= i).astype(jnp.int32)) for i in range(3)]
    for mine in range(own):
        rows = slice(mine * slab, (mine + 1) * slab)
        for layer, (q_ref, g_ref) in enumerate(((q_first, g_first), (q_second, g_second))):
            for head in range(heads):
                at = (layer * heads + head) * slab
                cols = slice(head * HD, (head + 1) * HD)
                q_rows[mine, at : at + slab, :] = q_ref[rows, cols]
                g_rows[mine, at : at + slab, :] = g_ref[rows, cols]
    order_copy.wait()
    for i in range(slabs, PLACES):
        facts[i] = 0
    for i in range(slabs):
        facts[order_ref[i]] = i // own * 2 * own + i % own
    first_slab = lax.axis_index("ctx") * own

    def dq_copies(mine):
        rows = pl.ds(pl.multiple_of(mine * slab, slab), slab)
        return [
            pltpu.make_async_copy(dq_stage.at[layer, rows], out.at[rows], dq_sems.at[mine, layer])
            for layer, out in enumerate((dq_first, dq_second))
        ]

    def one_slab(mine, carried):
        pos0 = order_ref[first_slab + mine] * slab
        row_pos = pos0 + (lax.broadcasted_iota(jnp.int32, (1, HD), 1) & (slab - 1))
        row_doc = jnp.zeros((1, HD), jnp.int32)
        low = jnp.int32(0)
        for bound in bounds:
            row_doc = jnp.where(row_pos >= bound, bound, row_doc)
            low = jnp.where(pos0 >= bound, bound, low)
        low = low // slab
        out_rows = pl.ds(pl.multiple_of(mine * slab, slab), slab)

        def work(size):
            q, g = q_rows[mine], g_rows[mine]
            top = jnp.full((1, width), MASKED_SCORE, jnp.float32)
            norm = weighted = jnp.zeros((1, width), jnp.float32)
            for start, part in chunks(size):
                key_pos = low * slab + start + lax.broadcasted_iota(jnp.int32, (part, HD), 0)
                allowed = (key_pos <= row_pos) & (key_pos >= row_doc)
                allowed = jnp.concatenate([allowed] * (width // HD), axis=1)
                at = places(facts, low, start, part, slab)
                rows = slice(start, start + part)
                keys = jnp.concatenate([kv_ref[pl.ds(a, slab), :] for a in at], axis=0)
                values = jnp.concatenate(
                    [kv_ref[pl.ds(a + own * slab, slab), :] for a in at], axis=0
                )
                s = jnp.where(allowed, dot(keys, q, NT) * scale2, MASKED_SCORE)
                scores_ref[rows, :] = s
                dp = dot(values, g, NT)
                grads_ref[rows, :] = dp
                new_top = jnp.maximum(top, jnp.max(s, axis=0, keepdims=True))
                e = jnp.exp2(s - new_top)
                fix = jnp.exp2(top - new_top)
                norm = norm * fix + jnp.sum(e, axis=0, keepdims=True)
                weighted = weighted * fix + jnp.sum(e * dp, axis=0, keepdims=True)
                top = new_top
            lse = top + jnp.log2(norm)
            delta = weighted / norm
            for start, part in chunks(size):
                at = places(facts, low, start, part, slab)
                rows = slice(start, start + part)
                p = jnp.exp2(scores_ref[rows, :] - lse)
                ds = (p * (grads_ref[rows, :] - delta)).astype(jnp.bfloat16)
                ds_ref[rows, :] = ds
                dv = dot(p.astype(jnp.bfloat16), g, NN)
                dk = dot(ds, q, NN)
                for j, a in enumerate(at):
                    piece = slice(j * slab, (j + 1) * slab)
                    key_sum[pl.ds(a, slab), :] += dk[piece] * scale
                    key_sum[pl.ds(a + own * slab, slab), :] += dv[piece]
            at = places(facts, low, 0, size, slab)
            keys = jnp.concatenate([kv_ref[pl.ds(a, slab), :] for a in at], axis=0)
            dq = (dot(keys.T, ds_ref[:size, :], NN) * scale).T.astype(jnp.bfloat16)
            for layer in range(2):
                for head in range(heads):
                    at = (layer * heads + head) * slab
                    cols = slice(head * HD, (head + 1) * HD)
                    dq_stage[layer, out_rows, cols] = dq[at : at + slab, :]

        for_size(pos0 + slab - low * slab, work)
        for copy in dq_copies(mine):
            copy.start()
        return carried

    lax.fori_loop(0, own, one_slab, 0)
    kvg_ref[...] = key_sum[...].astype(jnp.bfloat16)
    for mine in range(own):
        for copy in dq_copies(mine):
            copy.wait()


def attention(slab_order, doc_ids, q_first, q_second, g_first, g_second, kv):
    rows, width = q_first.shape
    slab = kv.shape[0] // (2 * slab_order.shape[0])
    own = rows // slab
    cols = 2 * (width // HD) * slab
    most = SIZES[-1]
    out = jax.ShapeDtypeStruct((rows, width), jnp.bfloat16)
    vmem = pl.BlockSpec(memory_space=pltpu.VMEM)
    hbm = pl.BlockSpec(memory_space=pltpu.HBM)
    slab_order = pltpu.with_memory_space_constraint(slab_order, pltpu.HBM)
    return pl.pallas_call(
        attention_kernel,
        out_shape=(out, out, jax.ShapeDtypeStruct(kv.shape, jnp.bfloat16)),
        in_specs=[hbm] + [vmem] * 6,
        out_specs=(hbm, hbm, vmem),
        scratch_shapes=[
            pltpu.SMEM(slab_order.shape, jnp.int32),
            pltpu.SMEM((PLACES,), jnp.int32),
            pltpu.VMEM((own, cols, HD), jnp.bfloat16),
            pltpu.VMEM((own, cols, HD), jnp.bfloat16),
            pltpu.VMEM((most, cols), jnp.float32),
            pltpu.VMEM((most, cols), jnp.float32),
            pltpu.VMEM((most, cols), jnp.bfloat16),
            pltpu.VMEM(kv.shape, jnp.float32),
            pltpu.VMEM((2, rows, width), jnp.bfloat16),
            pltpu.SemaphoreType.DMA(()),
            pltpu.SemaphoreType.DMA((own, 2)),
        ],
        compiler_params=pltpu.CompilerParams(vmem_limit_bytes=32 * 1024 * 1024),
    )(slab_order, doc_ids.reshape(-1, HD), q_first, q_second, g_first, g_second, kv)


SIDE = 4
ALONG_X = [[x * SIDE + y for x in range(SIDE)] for y in range(SIDE)]
ALONG_Y = [[x * SIDE + y for y in range(SIDE)] for x in range(SIDE)]


def exchange(blocks, groups):
    return lax.all_to_all(blocks, "ctx", 0, 0, axis_index_groups=groups)


def spread(block, groups):
    copies = jnp.broadcast_to(block[None], (SIDE,) + block.shape)
    return exchange(copies, groups).reshape(SIDE * block.shape[0], block.shape[1])


def per_device(
    slab_order,
    doc_ids,
    query_first,
    query_second,
    shared_keys,
    shared_values,
    out_grad_first,
    out_grad_second,
):
    kv = jnp.concatenate([shared_keys, shared_values], axis=0)
    kv = spread(spread(kv, ALONG_Y), ALONG_X)
    dq_first, dq_second, terms = attention(
        slab_order, doc_ids, query_first, query_second, out_grad_first, out_grad_second, kv
    )
    rows = shared_keys.shape[0]
    parts = exchange(terms.reshape(SIDE, -1, HD), ALONG_X)
    summed = jnp.sum(parts.astype(jnp.float32), axis=0).astype(jnp.bfloat16)
    parts = exchange(summed.reshape(SIDE, -1, HD), ALONG_Y)
    dk = jnp.sum(parts[:, :rows].astype(jnp.float32), axis=0).astype(jnp.bfloat16)
    dv = jnp.sum(parts[:, rows:].astype(jnp.float32), axis=0).astype(jnp.bfloat16)
    return (dq_first, dq_second, dk, dv)


def solution(mesh):
    rows = P(("dp", "ctx"), "head")
    return jax.shard_map(
        per_device,
        mesh=mesh,
        in_specs=(P("dp"), P("dp")) + (rows,) * 6,
        out_specs=(rows,) * 4,
        check_vma=False,
    )
```
